32 devices in a mesh: dp: 4 (over y, x), row: 4 (over z), col: 2 (over core).
Axes of the slice: x: 2, y: 2, z: 4, core: 2. Of those that a mesh axis runs over, the one named last changes fastest.
Arguments:
- tokens_in: bfloat16 [1024, 12288], P(('dp', 'col'), 'row'), may hold values from -28 to 28
- out_grad: bfloat16 [1024, 49152], P('dp', 'col'), may hold values from -8 to 8
- row_state: float32 [12288], P('row'), as said below
- col_state: float32 [49152], P(('col', 'dp')), as said below
Outputs:
- update: float32 [12288, 49152], P('row', ('col', 'dp'))
- row_stats: float32 [12288], P('row')
- col_stats: float32 [49152], P(('col', 'dp'))
The draws below stay inside these ranges and needn't reach their ends.
Inputs may be any that keep to these rules, and one draw needn't show every extreme that they name: `row_state`: positive. `col_state`: positive.
All inputs are finite; a program needn't handle non-finite values.
Results may differ from the reference program's by a relative error of at most 0.0003.
Values may be sent and summed in bfloat16 or wider, within the bound.
A program may use at most 192 MiB of HBM per device.

```python
import math
import jax
import jax.numpy as jnp
from jax import lax

D = 12288
F = 49152
TOKENS = 1024
N_DP = 4
N_COL = 2


def scales(key, label, length, spread):
    inner = jax.random.fold_in(key, label)
    rough = jax.random.uniform(inner, (length,), jnp.float32)
    place = (jnp.arange(length, dtype=jnp.float32) + 0.5) / length
    return jnp.exp(math.log(3.0) * (place - 0.5) + math.log(spread) * (rough - 0.5))


def levels(key, length):
    rough = jax.random.uniform(key, (length,), jnp.float32, math.log(0.1), 0.0)
    place = (jnp.arange(length, dtype=jnp.float32) + 0.5) / length
    return jnp.exp(rough - math.log(3.0) * (place - 0.5))


def falling(length, blocks, groups, ratio):
    width = length // (blocks * groups)
    group_index = jnp.arange(length, dtype=jnp.int32) // width % groups
    share = group_index.astype(jnp.float32) / max(groups - 1, 1)
    return jnp.exp(-math.log(ratio) * share)


def draw_tokens_in(key, part):
    feature = scales(key, 101, D, 10.0)
    key = jax.random.fold_in(key, 1)
    values = jnp.clip(jax.random.normal(key, (TOKENS, D), jnp.float32), -4.0, 4.0)
    return (values * feature[None, :]).astype(jnp.bfloat16)


def draw_out_grad(key, part):
    feature = scales(key, 202, F, 10.0)
    key = jax.random.fold_in(key, 2)
    values = jnp.clip(jax.random.normal(key, (TOKENS, F), jnp.float32), -4.0, 4.0)
    values = values * feature[None, :] / math.sqrt(TOKENS)
    return jnp.clip(values, -8.0, 8.0).astype(jnp.bfloat16)


def draw_row_state(key, part):
    feature = scales(key, 101, D, 10.0)
    key = jax.random.fold_in(key, 3)
    return (feature * feature * 2.6 * levels(key, D)).astype(jnp.float32)


def draw_col_state(key, part):
    feature = scales(key, 202, F, 10.0)
    tilt = falling(F, N_COL, N_DP, 6.0)
    key = jax.random.fold_in(key, 4)
    return (feature * feature * 2.6 * levels(key, F) * tilt).astype(jnp.float32)


def setup_inputs(seed: int = 0) -> dict:
    arg_keys = jax.random.split(jax.random.key(seed), 5)
    tokens_in = draw_tokens_in(jax.random.fold_in(arg_keys[4], 71), 0)
    out_grad = draw_out_grad(jax.random.fold_in(arg_keys[4], 71), 0)
    row_state = draw_row_state(jax.random.fold_in(arg_keys[4], 71), 0)
    col_state = draw_col_state(jax.random.fold_in(arg_keys[4], 71), 0)
    return dict(tokens_in=tokens_in, out_grad=out_grad, row_state=row_state, col_state=col_state)


DECAY = 0.7
CLIP = 1.0

def reference(tokens_in, out_grad, row_state, col_state):
    weight_grad = jnp.dot(tokens_in.T, out_grad, preferred_element_type=jnp.float32)
    squared = weight_grad * weight_grad
    row_stats = DECAY * row_state + (1.0 - DECAY) * (lax.optimization_barrier(jnp.sum(squared, axis=1)) / F)
    col_stats = DECAY * col_state + (1.0 - DECAY) * (lax.optimization_barrier(jnp.sum(squared, axis=0)) / D)
    row_mean = jnp.sum(row_stats) / D
    raw_update = weight_grad * lax.rsqrt(row_stats / row_mean)[:, None] * lax.rsqrt(col_stats)[None, :]
    power_mean = jnp.sum(raw_update * raw_update) / (D * F)
    clip_factor = jnp.maximum(1.0, jnp.sqrt(power_mean) / CLIP)
    return (raw_update / clip_factor, row_stats, col_stats)
```

```python
import functools

import jax
import jax.numpy as jnp
from jax import lax
from jax.experimental import pallas as pl
from jax.experimental.pallas import tpu as pltpu
from jax.sharding import PartitionSpec as P

MESH = pl.DeviceIdType.MESH
DECAY = 0.7
CLIP = 1.0
LANES = 128
AHEAD = 2
FLIGHT = 3


def gather_kernel(sizes, tok_ref, og_ref, rstate_ref, cstate_ref,
                  g_ref, x_ref, xt_out, wgs_ref, ra_ref, cb_ref, rstat_ref, cstat_ref,
                  xt, gbuf, hold, stage, colacc, rslot, r2slot, cslot, pslot, qslot, p2slot,
                  xs, xr, zs, zr, ts, tr, us, ur, es, er, lsem, stsem, gsem):
    n_dp, n_row, n_col, cw, rt = sizes
    R = xt.shape[0]
    W = g_ref.shape[1]
    T = og_ref.shape[0]
    half = T // 2
    tb = tok_ref.shape[0]
    nch = W // cw
    groups = cw // LANES
    dp, row, col = lax.axis_index("dp"), lax.axis_index("row"), lax.axis_index("col")
    h = row % 2
    mate = row + 1 - 2 * h

    def peer(i, d, n):
        return lax.rem(i + d, n)

    def origin(i, d, n):
        return lax.rem(i + n - d, n)

    def mul(v, m):
        return pl.multiple_of(v * m, m)

    barrier = pltpu.get_barrier_semaphore()
    for axis, me, n in (("dp", dp, n_dp), ("row", row, n_row), ("col", col, n_col)):
        for d in range(1, n):
            pl.semaphore_signal(barrier, inc=1, device_id={axis: peer(me, d, n)}, device_id_type=MESH)
    pl.semaphore_wait(barrier, n_dp + n_row + n_col - 3)

    def xy(k, d):
        to = peer(dp, d, n_dp)
        return pltpu.make_async_remote_copy(
            src_ref=og_ref.at[pl.ds(mul(h, half), half), pl.ds(pl.multiple_of(to * W + k * cw, LANES), cw)],
            dst_ref=g_ref.at[pl.ds(pl.multiple_of(dp * T + h * half, half), half), pl.ds(mul(k, cw), cw)],
            send_sem=xs.at[k, d - 1], recv_sem=xr.at[k, d - 1],
            device_id={"dp": to}, device_id_type=MESH)

    def block(k, d, part):
        frm = origin(dp, d, n_dp)
        return g_ref.at[pl.ds(pl.multiple_of(frm * T + part * half, half), half), pl.ds(mul(k, cw), cw)]

    def xy_in(k, d):
        ref = block(k, d, h)
        return pltpu.make_async_remote_copy(
            src_ref=ref, dst_ref=ref, send_sem=xs.at[k, d - 1], recv_sem=xr.at[k, d - 1],
            device_id={"dp": origin(dp, d, n_dp)}, device_id_type=MESH)

    def zcopy(k, d, part):
        ref = block(k, d, part)
        return pltpu.make_async_remote_copy(
            src_ref=ref, dst_ref=ref, send_sem=zs.at[k, d - 1], recv_sem=zr.at[k, d - 1],
            device_id={"row": mate}, device_id_type=MESH)

    def send_xy(k):
        for d in range(1, n_dp):
            xy(k, d).start()

    def forward(k):
        for d in range(1, n_dp):
            xy_in(k, d).wait_recv()
            zcopy(k, d, h).start()

    def next_send(k):
        for d in range(1, n_dp):
            xy(k, d).wait_send()

        @pl.when(k + FLIGHT < nch)
        def _():
            send_xy(k + FLIGHT)

    def tokens_at(i, c):
        return x_ref.at[pl.ds(mul(i * n_col + c, tb), tb), :]

    def tok_dp(d, frm):
        ref = tokens_at(frm, col)
        return pltpu.make_async_remote_copy(
            src_ref=tok_ref, dst_ref=ref, send_sem=ts.at[d - 1], recv_sem=tr.at[d - 1],
            device_id={"dp": peer(dp, d, n_dp)}, device_id_type=MESH)

    def tok_col(d, e, c):
        ref = tokens_at(origin(dp, d, n_dp), c)
        return pltpu.make_async_remote_copy(
            src_ref=tok_ref if d == 0 else ref, dst_ref=ref, send_sem=us.at[d, e - 1], recv_sem=ur.at[d, e - 1],
            device_id={"col": peer(col, e, n_col)}, device_id_type=MESH)

    own_tok = pltpu.make_async_copy(tok_ref, tokens_at(dp, col), lsem.at[0])
    own_tok.start()
    own_grad = pltpu.make_async_copy(
        og_ref.at[:, pl.ds(mul(dp, W), W)], g_ref.at[pl.ds(mul(dp, T), T), :], lsem.at[1])
    own_grad.start()
    send_xy(0)
    for d in range(1, n_dp):
        tok_dp(d, dp).start()
    for e in range(1, n_col):
        tok_col(0, e, col).start()
    for k in range(1, min(FLIGHT, nch)):
        send_xy(k)

    ra_ref[...] = jnp.zeros_like(ra_ref)
    colacc[...] = jnp.zeros_like(colacc)

    forward(0)
    next_send(0)
    for d in range(1, n_dp):
        tok_dp(d, origin(dp, d, n_dp)).wait_recv()
        for e in range(1, n_col):
            tok_col(d, e, col).start()
    for k in range(1, min(AHEAD, nch)):
        forward(k)
        next_send(k)
    own_tok.wait()
    for d in range(n_dp):
        for e in range(1, n_col):
            tok_col(d, e, origin(col, e, n_col)).wait_recv()

    def load_x(q, slot):
        return pltpu.make_async_copy(x_ref.at[:, pl.ds(mul(q, cw), cw)], gbuf.at[slot], gsem.at[slot])

    load_x(0, 0).start()

    @pl.loop(0, R // cw)
    def _(q):
        slot = q % 2
        load_x(q, slot).wait()

        @pl.when(q + 1 < R // cw)
        def _():
            load_x(q + 1, 1 - slot).start()

        for part in range(groups):
            xt[pl.ds(pl.multiple_of(q * cw + part * LANES, LANES), LANES), :] = (
                gbuf[slot, :, part * LANES:(part + 1) * LANES].T)

    out_xt = pltpu.make_async_copy(xt, xt_out, lsem.at[2])
    out_xt.start()
    own_grad.wait()

    def work(k, save):
        load = pltpu.make_async_copy(g_ref.at[:, pl.ds(mul(k, cw), cw)], gbuf.at[0], gsem.at[0])
        load.start()
        load.wait()
        columns = pl.ds(mul(k, cw), cw)

        @pl.loop(0, R // rt)
        def _(r):
            rows = pl.ds(mul(r, rt), rt)
            w = jnp.dot(xt[rows, :], gbuf[0], preferred_element_type=jnp.float32)
            save(r, w)
            sq = w * w
            part = sq[:, :LANES]
            for j in range(1, groups):
                part = part + sq[:, j * LANES:(j + 1) * LANES]
            ra_ref[rows, :] += part
            colacc[:, columns] += jnp.sum(sq.reshape(rt // 8, 8, cw), axis=0)

    def arrive(k):
        @pl.when(k + AHEAD < nch)
        def _():
            forward(k + AHEAD)
            next_send(k + AHEAD)

        for d in range(1, n_dp):
            zcopy(k, d, 1 - h).wait_recv()

    def store_out(p, s):
        return pltpu.make_async_copy(
            stage.at[s], wgs_ref.at[pl.ds(s * (R // 2), R // 2), pl.ds(mul(p, cw), cw)], stsem.at[s])

    def load_back(p, s):
        return pltpu.make_async_copy(
            wgs_ref.at[pl.ds(s * (R // 2), R // 2), pl.ds(mul(p, cw), cw)], stage.at[s], stsem.at[s])

    tiles = R // 2 // rt

    @pl.loop(0, nch // 2)
    def _(p):
        arrive(2 * p)

        @pl.when(p > 0)
        def _():
            for s in range(2):
                store_out(p - 1, s).wait()

        def to_stage(r, w):
            stage[r // tiles, pl.ds(mul(r % tiles, rt), rt), :] = w

        work(2 * p, to_stage)
        for s in range(2):
            store_out(p, s).start()
        arrive(2 * p + 1)

        def to_hold(r, w):
            hold[p, pl.ds(mul(r, rt), rt), :] = w

        work(2 * p + 1, to_hold)

    def exchange(axis, me, n, slots, row_no):
        out = []
        for d in range(1, n):
            c = pltpu.make_async_remote_copy(
                src_ref=slots.at[me], dst_ref=slots.at[me], send_sem=es.at[row_no, d - 1],
                recv_sem=er.at[row_no, d - 1], device_id={axis: peer(me, d, n)}, device_id_type=MESH)
            c.start()
            out.append(c)

        def finish():
            for d in range(1, n):
                ref = slots.at[origin(me, d, n)]
                out[d - 1].wait_send()
                pltpu.make_async_remote_copy(
                    src_ref=ref, dst_ref=ref, send_sem=es.at[row_no, d - 1], recv_sem=er.at[row_no, d - 1],
                    device_id={axis: peer(me, d, n)}, device_id_type=MESH).wait_recv()
            total = slots[0]
            for i in range(1, n):
                total = total + slots[i]
            return total

        return finish

    nb = R // LANES
    cslot[row] = jnp.sum(colacc[...], axis=0, keepdims=True)
    finish_col = exchange("row", row, n_row, cslot, 0)
    for b in range(nb):
        rslot[dp, b:b + 1, :] = jnp.sum(ra_ref[b * LANES:(b + 1) * LANES, :].T, axis=0, keepdims=True)
    r2slot[col] = exchange("dp", dp, n_dp, rslot, 1)()
    row_sum = exchange("col", col, n_col, r2slot, 2)()
    row_stats = DECAY * rstate_ref[...] + (1.0 - DECAY) * (row_sum / (W * n_dp * n_col))
    rstat_ref[...] = row_stats
    local_mean = jnp.sum(row_stats) / R
    scale = lax.rsqrt(row_stats / local_mean)
    for b in range(nb):
        ra_ref[b * LANES:(b + 1) * LANES, :] = jnp.broadcast_to(scale[b:b + 1, :], (LANES, LANES)).T
    col_stats = DECAY * cstate_ref[...] + (1.0 - DECAY) * (finish_col() / (R * n_row))
    cstat_ref[...] = col_stats
    cb_ref[...] = lax.rsqrt(col_stats)

    for s in range(2):
        store_out(nch // 2 - 1, s).wait()
    pslot[dp] = jnp.zeros((8, LANES), jnp.float32)

    def power(read, first, count, k):
        columns = pl.ds(mul(k, cw), cw)
        cb = cb_ref[:, columns]

        @pl.loop(0, count)
        def _(r):
            a = ra_ref[pl.ds(pl.multiple_of(first + r * rt, rt), rt), :]
            w = read(r)
            acc = jnp.zeros((8, LANES), jnp.float32)
            for j in range(groups):
                u = w[:, j * LANES:(j + 1) * LANES] * a * cb[:, j * LANES:(j + 1) * LANES]
                acc = acc + jnp.sum((u * u).reshape(rt // 8, 8, LANES), axis=0)
            pslot[dp] += acc

    for s in range(2):
        load_back(0, s).start()

    @pl.loop(0, nch // 2)
    def _(p):
        power(lambda r: hold[p, pl.ds(mul(r, rt), rt), :], 0, R // rt, 2 * p + 1)
        for s in range(2):
            load_back(p, s).wait()
            power(lambda r: stage[s, pl.ds(mul(r, rt), rt), :], s * (R // 2), tiles, 2 * p)

            @pl.when(p + 1 < nch // 2)
            def _():
                load_back(p + 1, s).start()

    qslot[row, 0:8, :] = exchange("dp", dp, n_dp, pslot, 3)()
    qslot[row, 8:16, :] = jnp.full((8, LANES), local_mean, jnp.float32)
    exchange("row", row, n_row, qslot, 4)()
    mean = qslot[0, 8:16, :]
    for i in range(1, n_row):
        mean = mean + qslot[i, 8:16, :]
    mean = mean / n_row
    total = qslot[0, 0:8, :] * (mean / qslot[0, 8:16, :])
    for i in range(1, n_row):
        total = total + qslot[i, 0:8, :] * (mean / qslot[i, 8:16, :])
    p2slot[col] = total
    power_mean = jnp.sum(exchange("col", col, n_col, p2slot, 5)()) / (R * n_row * W * n_dp * n_col)
    tail = jnp.full((1, LANES), power_mean, jnp.float32)
    clip = jnp.maximum(1.0, jnp.sqrt(tail) / CLIP)
    factor = jnp.sqrt(mean[0:1, :] / local_mean) / clip
    for j in range(W // LANES):
        cb_ref[:, j * LANES:(j + 1) * LANES] = cb_ref[:, j * LANES:(j + 1) * LANES] * factor

    out_xt.wait()
    for d in range(1, n_dp):
        tok_dp(d, dp).wait_send()
    for d in range(n_dp):
        for e in range(1, n_col):
            tok_col(d, e, col).wait_send()

    @pl.loop(0, nch)
    def _(k):
        for d in range(1, n_dp):
            zcopy(k, d, h).wait_send()


def finish_kernel(xt_ref, g_ref, w_ref, ra_ref, cb_ref, out_ref):
    rows, cw = w_ref.shape
    r = pl.program_id(1)
    a = ra_ref[...]
    cb = cb_ref[...]
    x = xt_ref[pl.ds(pl.multiple_of(r * rows, rows), rows), :]
    w = jnp.dot(x, g_ref[...], preferred_element_type=jnp.float32)
    for j in range(cw // LANES):
        s = slice(j * LANES, (j + 1) * LANES)
        out_ref[:, s] = w_ref[:, s] * a * cb[:, s]
        s2 = slice(cw + j * LANES, cw + (j + 1) * LANES)
        out_ref[:, s2] = w[:, s] * a * cb[:, s2]


def on_device(sizes, tokens_in, out_grad, row_state, col_state):
    n_dp, n_row, n_col = sizes
    tb, R = tokens_in.shape
    T, wide = out_grad.shape
    W = wide // n_dp
    tokens = T * n_dp
    cw = 512 if W % 1024 == 0 else W // 2
    rt = 256
    nch = W // cw
    nb = R // LANES
    f32, bf16 = jnp.float32, jnp.bfloat16
    anywhere = pl.BlockSpec(memory_space=pl.ANY)
    vmem = pl.BlockSpec(memory_space=pltpu.VMEM)
    dma = pltpu.SemaphoreType.DMA
    peers = max(n_dp, n_row, n_col) - 1
    g, _, xt, wgs, ra, cb, row_stats, col_stats = pl.pallas_call(
        functools.partial(gather_kernel, (n_dp, n_row, n_col, cw, rt)),
        out_shape=[
            jax.ShapeDtypeStruct((tokens, W), bf16),
            jax.ShapeDtypeStruct((tokens, R), bf16),
            jax.ShapeDtypeStruct((R, tokens), bf16),
            jax.ShapeDtypeStruct((R, W // 2), f32),
            jax.ShapeDtypeStruct((R, LANES), f32),
            jax.ShapeDtypeStruct((1, W), f32),
            jax.ShapeDtypeStruct((nb, LANES), f32),
            jax.ShapeDtypeStruct((1, W), f32),
        ],
        in_specs=[anywhere, anywhere, vmem, vmem],
        out_specs=[anywhere] * 4 + [vmem] * 4,
        scratch_shapes=[
            pltpu.VMEM((R, tokens), bf16),
            pltpu.VMEM((2, tokens, cw), bf16),
            pltpu.VMEM((nch // 2, R, cw), f32),
            pltpu.VMEM((2, R // 2, cw), f32),
            pltpu.VMEM((8, W), f32),
            pltpu.VMEM((n_dp, nb, LANES), f32),
            pltpu.VMEM((n_col, nb, LANES), f32),
            pltpu.VMEM((n_row, 1, W), f32),
            pltpu.VMEM((n_dp, 8, LANES), f32),
            pltpu.VMEM((n_row, 16, LANES), f32),
            pltpu.VMEM((n_col, 8, LANES), f32),
            dma((nch, n_dp - 1)), dma((nch, n_dp - 1)), dma((nch, n_dp - 1)), dma((nch, n_dp - 1)),
            dma((n_dp - 1,)), dma((n_dp - 1,)),
            dma((n_dp, n_col - 1)), dma((n_dp, n_col - 1)),
            dma((6, peers)), dma((6, peers)),
            dma((3,)), dma((2,)), dma((2,)),
        ],
        compiler_params=pltpu.CompilerParams(
            collective_id=0, has_side_effects=True, vmem_limit_bytes=60 * 1024 * 1024),
        cost_estimate=pl.CostEstimate(flops=2 * R * W * tokens, bytes_accessed=8 * R * W, transcendentals=0),
        name="exchange_and_stats",
    )(tokens_in, out_grad, row_state.reshape(nb, LANES), col_state.reshape(1, W))

    frt = 512
    update = pl.pallas_call(
        finish_kernel,
        out_shape=jax.ShapeDtypeStruct((R, W), f32),
        grid=(nch // 2, R // frt),
        in_specs=[
            pl.BlockSpec(memory_space=pltpu.VMEM),
            pl.BlockSpec((tokens, cw), lambda p, r: (0, 2 * p + 1)),
            pl.BlockSpec((frt, cw), lambda p, r: (r, p)),
            pl.BlockSpec((frt, LANES), lambda p, r: (r, 0)),
            pl.BlockSpec((1, 2 * cw), lambda p, r: (0, p)),
        ],
        out_specs=pl.BlockSpec((frt, 2 * cw), lambda p, r: (r, p)),
        compiler_params=pltpu.CompilerParams(vmem_limit_bytes=48 * 1024 * 1024),
        cost_estimate=pl.CostEstimate(flops=R * W * tokens, bytes_accessed=6 * R * W, transcendentals=0),
        name="scaled_update",
    )(xt, g, wgs, ra, cb)
    return update, row_stats.reshape(R), col_stats.reshape(W)


def solution(mesh):
    sizes = (mesh.shape["dp"], mesh.shape["row"], mesh.shape["col"])
    return jax.shard_map(
        functools.partial(on_device, sizes),
        mesh=mesh,
        in_specs=(P(("dp", "col"), "row"), P("dp", "col"), P("row"), P(("col", "dp"))),
        out_specs=(P("row", ("col", "dp")), P("row"), P(("col", "dp"))),
        check_vma=False,
    )
```

```python
import functools

import jax
import jax.numpy as jnp
from jax import lax
from jax.experimental import pallas as pl
from jax.experimental.pallas import tpu as pltpu
from jax.sharding import PartitionSpec as P

MESH = pl.DeviceIdType.MESH
DECAY = 0.7
CLIP = 1.0
LANES = 128
AHEAD = 3
FLIGHT = 3


def gather_kernel(sizes, tok_ref, og_ref, rstate_ref, cstate_ref,
                  g_ref, x_ref, xt_out, wgs_ref, ra_ref, cb_ref, rstat_ref, cstat_ref,
                  xt, gbuf, hold, stage, colacc, rslot, r2slot, cslot, pslot, qslot, p2slot,
                  xs, xr, zs, zr, ts, tr, us, ur, es, er, lsem, stsem, gsem):
    n_dp, n_row, n_col, cw, rt = sizes
    R = xt.shape[0]
    W = g_ref.shape[1]
    T = og_ref.shape[0]
    half = T // 2
    tb = tok_ref.shape[0]
    nch = W // cw
    groups = cw // LANES
    wide = 2 * cw
    pieces = R // wide
    shared = nch - nch // 6
    dp, row, col = lax.axis_index("dp"), lax.axis_index("row"), lax.axis_index("col")
    h = row % 2
    mate = row + 1 - 2 * h

    def peer(i, d, n):
        return lax.rem(i + d, n)

    def origin(i, d, n):
        return lax.rem(i + n - d, n)

    def mul(v, m):
        return pl.multiple_of(v * m, m)

    barrier = pltpu.get_barrier_semaphore()
    for axis, me, n in (("dp", dp, n_dp), ("row", row, n_row), ("col", col, n_col)):
        for d in range(1, n):
            pl.semaphore_signal(barrier, inc=1, device_id={axis: peer(me, d, n)}, device_id_type=MESH)
    pl.semaphore_wait(barrier, n_dp + n_row + n_col - 3)

    def xy(k, d, part, ss, rs):
        to = peer(dp, d, n_dp)
        return pltpu.make_async_remote_copy(
            src_ref=og_ref.at[pl.ds(mul(part, half), half), pl.ds(pl.multiple_of(to * W + k * cw, LANES), cw)],
            dst_ref=g_ref.at[pl.ds(pl.multiple_of(dp * T + part * half, half), half), pl.ds(mul(k, cw), cw)],
            send_sem=ss.at[k, d - 1], recv_sem=rs.at[k, d - 1],
            device_id={"dp": to}, device_id_type=MESH)

    def block(k, d, part):
        frm = origin(dp, d, n_dp)
        return g_ref.at[pl.ds(pl.multiple_of(frm * T + part * half, half), half), pl.ds(mul(k, cw), cw)]

    def xy_in(k, d):
        ref = block(k, d, h)
        return pltpu.make_async_remote_copy(
            src_ref=ref, dst_ref=ref, send_sem=xs.at[k, d - 1], recv_sem=xr.at[k, d - 1],
            device_id={"dp": origin(dp, d, n_dp)}, device_id_type=MESH)

    def zcopy(k, d, part):
        ref = block(k, d, part)
        return pltpu.make_async_remote_copy(
            src_ref=ref, dst_ref=ref, send_sem=zs.at[k, d - 1], recv_sem=zr.at[k, d - 1],
            device_id={"row": mate}, device_id_type=MESH)

    def send_xy(k):
        for d in range(1, n_dp):
            xy(k, d, h, xs, xr).start()

        @pl.when(k >= shared)
        def _():
            for d in range(1, n_dp):
                xy(k, d, 1 - h, zs, zr).start()

    def forward(k):
        for d in range(1, n_dp):
            xy_in(k, d).wait_recv()
            zcopy(k, d, h).start()

    def tokens_at(i, c, q):
        return x_ref.at[pl.ds(mul(i * n_col + c, tb), tb), pl.ds(q * wide, wide)]

    def tok_piece(q):
        return tok_ref.at[:, pl.ds(q * wide, wide)]

    def tok_dp(q, d, frm):
        return pltpu.make_async_remote_copy(
            src_ref=tok_piece(q), dst_ref=tokens_at(frm, col, q),
            send_sem=ts.at[q, d - 1], recv_sem=tr.at[q, d - 1],
            device_id={"dp": peer(dp, d, n_dp)}, device_id_type=MESH)

    def tok_col(q, d, e, c):
        ref = tokens_at(origin(dp, d, n_dp), c, q)
        return pltpu.make_async_remote_copy(
            src_ref=tok_piece(q) if d == 0 else ref, dst_ref=ref,
            send_sem=us.at[q * n_dp + d, e - 1], recv_sem=ur.at[q * n_dp + d, e - 1],
            device_id={"col": peer(col, e, n_col)}, device_id_type=MESH)

    def send_tok(q):
        for d in range(1, n_dp):
            tok_dp(q, d, dp).start()
        for e in range(1, n_col):
            tok_col(q, 0, e, col).start()

    def pass_tok(q):
        for d in range(1, n_dp):
            tok_dp(q, d, origin(dp, d, n_dp)).wait_recv()
            for e in range(1, n_col):
                tok_col(q, d, e, col).start()

    first = min(FLIGHT, nch)
    send_xy(0)
    own_tok = pltpu.make_async_copy(tok_ref, x_ref.at[pl.ds(mul(dp * n_col + col, tb), tb), :], lsem.at[0])
    own_tok.start()
    send_tok(0)
    own_grad = pltpu.make_async_copy(
        og_ref.at[:, pl.ds(mul(dp, W), W)], g_ref.at[pl.ds(mul(dp, T), T), :], lsem.at[1])
    own_grad.start()
    if first > 1:
        send_xy(1)

    ra_ref[...] = jnp.zeros_like(ra_ref)
    colacc[...] = jnp.zeros_like(colacc)

    def turn_tok(q):
        for d in range(n_dp):
            for e in range(1, n_col):
                tok_col(q, d, e, origin(col, e, n_col)).wait_recv()
        load = pltpu.make_async_copy(x_ref.at[:, pl.ds(q * wide, wide)], gbuf, gsem.at[0])
        load.start()
        load.wait()
        for part in range(wide // LANES):
            xt[q * wide + part * LANES:q * wide + (part + 1) * LANES, :] = (
                gbuf[:, part * LANES:(part + 1) * LANES].T)

    sent = min(2, nch)
    own_tok.wait()
    for q in range(pieces):
        if q + 1 < pieces:
            send_tok(q + 1)
        if q < min(AHEAD, shared):
            forward(q)
        if sent < nch:
            send_xy(sent)
            sent += 1
        pass_tok(q)
        if q > 0:
            turn_tok(q - 1)
    for q in range(pieces, min(AHEAD, shared)):
        forward(q)
    turn_tok(pieces - 1)

    out_xt = pltpu.make_async_copy(xt, xt_out, lsem.at[2])
    out_xt.start()
    own_grad.wait()

    def work(p):
        load = pltpu.make_async_copy(g_ref.at[:, pl.ds(mul(p, wide), wide)], gbuf, gsem.at[0])
        load.start()
        load.wait()
        columns = pl.ds(mul(p, wide), wide)

        @pl.loop(0, R // rt)
        def _(r):
            rows = pl.ds(mul(r, rt), rt)
            w = jnp.dot(xt[rows, :], gbuf[...], preferred_element_type=jnp.float32)
            stage[r // tiles, pl.ds(mul(r % tiles, rt), rt), :] = w[:, :cw]
            hold[p, rows, :] = w[:, cw:]
            sq = w * w
            part = sq[:, :LANES]
            for j in range(1, 2 * groups):
                part = part + sq[:, j * LANES:(j + 1) * LANES]
            ra_ref[rows, :] += part
            colacc[:, columns] += jnp.sum(sq.reshape(rt // 8, 8, wide), axis=0)

    def arrive(p):
        for i in range(2):
            k = 2 * p + i

            @pl.when(k + AHEAD < shared)
            def _():
                forward(k + AHEAD)

            @pl.when(k + sent < nch)
            def _():
                send_xy(k + sent)

        for i in range(2):
            k = 2 * p + i
            for d in range(1, n_dp):
                zcopy(k, d, 1 - h).wait_recv()

            @pl.when(k >= shared)
            def _():
                for d in range(1, n_dp):
                    xy_in(k, d).wait_recv()

    tiles = R // 2 // rt

    def store_out(p, s):
        return pltpu.make_async_copy(
            stage.at[s], wgs_ref.at[pl.ds(s * (R // 2), R // 2), pl.ds(mul(p, cw), cw)], stsem.at[s])

    def load_back(p, s):
        return pltpu.make_async_copy(
            wgs_ref.at[pl.ds(s * (R // 2), R // 2), pl.ds(mul(p, cw), cw)], stage.at[s], stsem.at[s])

    @pl.loop(0, nch // 2)
    def _(p):
        arrive(p)

        @pl.when(p > 0)
        def _():
            for s in range(2):
                store_out(p - 1, s).wait()

        work(p)
        for s in range(2):
            store_out(p, s).start()

    def exchange(axis, me, n, slots, row_no):
        out = []
        for d in range(1, n):
            c = pltpu.make_async_remote_copy(
                src_ref=slots.at[me], dst_ref=slots.at[me], send_sem=es.at[row_no, d - 1],
                recv_sem=er.at[row_no, d - 1], device_id={axis: peer(me, d, n)}, device_id_type=MESH)
            c.start()
            out.append(c)

        def finish():
            for d in range(1, n):
                ref = slots.at[origin(me, d, n)]
                out[d - 1].wait_send()
                pltpu.make_async_remote_copy(
                    src_ref=ref, dst_ref=ref, send_sem=es.at[row_no, d - 1], recv_sem=er.at[row_no, d - 1],
                    device_id={axis: peer(me, d, n)}, device_id_type=MESH).wait_recv()
            total = slots[0]
            for i in range(1, n):
                total = total + slots[i]
            return total

        return finish

    nb = R // LANES
    cslot[row] = jnp.sum(colacc[...], axis=0, keepdims=True)
    finish_col = exchange("row", row, n_row, cslot, 0)
    for b in range(nb):
        rslot[dp, b:b + 1, :] = jnp.sum(ra_ref[b * LANES:(b + 1) * LANES, :].T, axis=0, keepdims=True)
    r2slot[col] = exchange("dp", dp, n_dp, rslot, 1)()
    row_sum = exchange("col", col, n_col, r2slot, 2)()
    row_stats = DECAY * rstate_ref[...] + (1.0 - DECAY) * (row_sum / (W * n_dp * n_col))
    rstat_ref[...] = row_stats
    local_mean = jnp.sum(row_stats) / R
    scale = lax.rsqrt(row_stats / local_mean)
    for b in range(nb):
        ra_ref[b * LANES:(b + 1) * LANES, :] = jnp.broadcast_to(scale[b:b + 1, :], (LANES, LANES)).T
    col_stats = DECAY * cstate_ref[...] + (1.0 - DECAY) * (finish_col() / (R * n_row))
    cstat_ref[...] = col_stats
    cb_ref[...] = lax.rsqrt(col_stats)

    for s in range(2):
        store_out(nch // 2 - 1, s).wait()
    pslot[dp] = jnp.zeros((8, LANES), jnp.float32)

    def power(read, first, count, k):
        columns = pl.ds(mul(k, cw), cw)
        cb = cb_ref[:, columns]

        @pl.loop(0, count)
        def _(r):
            a = ra_ref[pl.ds(pl.multiple_of(first + r * rt, rt), rt), :]
            w = read(r)
            acc = jnp.zeros((8, LANES), jnp.float32)
            for j in range(groups):
                u = w[:, j * LANES:(j + 1) * LANES] * a * cb[:, j * LANES:(j + 1) * LANES]
                acc = acc + jnp.sum((u * u).reshape(rt // 8, 8, LANES), axis=0)
            pslot[dp] += acc

    for s in range(2):
        load_back(0, s).start()

    @pl.loop(0, nch // 2)
    def _(p):
        power(lambda r: hold[p, pl.ds(mul(r, rt), rt), :], 0, R // rt, 2 * p + 1)
        for s in range(2):
            load_back(p, s).wait()
            power(lambda r: stage[s, pl.ds(mul(r, rt), rt), :], s * (R // 2), tiles, 2 * p)

            @pl.when(p + 1 < nch // 2)
            def _():
                load_back(p + 1, s).start()

    qslot[row, 0:8, :] = exchange("dp", dp, n_dp, pslot, 3)()
    qslot[row, 8:16, :] = jnp.full((8, LANES), local_mean, jnp.float32)
    exchange("row", row, n_row, qslot, 4)()
    mean = qslot[0, 8:16, :]
    for i in range(1, n_row):
        mean = mean + qslot[i, 8:16, :]
    mean = mean / n_row
    total = qslot[0, 0:8, :] * (mean / qslot[0, 8:16, :])
    for i in range(1, n_row):
        total = total + qslot[i, 0:8, :] * (mean / qslot[i, 8:16, :])
    p2slot[col] = total
    power_mean = jnp.sum(exchange("col", col, n_col, p2slot, 5)()) / (R * n_row * W * n_dp * n_col)
    tail = jnp.full((1, LANES), power_mean, jnp.float32)
    clip = jnp.maximum(1.0, jnp.sqrt(tail) / CLIP)
    factor = jnp.sqrt(mean[0:1, :] / local_mean) / clip
    for j in range(W // LANES):
        cb_ref[:, j * LANES:(j + 1) * LANES] = cb_ref[:, j * LANES:(j + 1) * LANES] * factor

    out_xt.wait()
    for q in range(pieces):
        for d in range(1, n_dp):
            tok_dp(q, d, dp).wait_send()
        for d in range(n_dp):
            for e in range(1, n_col):
                tok_col(q, d, e, col).wait_send()

    @pl.loop(0, nch)
    def _(k):
        for d in range(1, n_dp):
            xy(k, d, h, xs, xr).wait_send()
            zcopy(k, d, h).wait_send()


def finish_kernel(xt_ref, g_ref, w_ref, ra_ref, cb_ref, out_ref):
    rows, cw = w_ref.shape
    r = pl.program_id(1)
    a = ra_ref[...]
    cb = cb_ref[...]
    x = xt_ref[pl.ds(pl.multiple_of(r * rows, rows), rows), :]
    w = jnp.dot(x, g_ref[...], preferred_element_type=jnp.float32)
    for j in range(cw // LANES):
        s = slice(j * LANES, (j + 1) * LANES)
        out_ref[:, s] = w_ref[:, s] * a * cb[:, s]
        s2 = slice(cw + j * LANES, cw + (j + 1) * LANES)
        out_ref[:, s2] = w[:, s] * a * cb[:, s2]


def on_device(sizes, tokens_in, out_grad, row_state, col_state):
    n_dp, n_row, n_col = sizes
    tb, R = tokens_in.shape
    T, wide = out_grad.shape
    W = wide // n_dp
    tokens = T * n_dp
    cw = 512 if W % 1024 == 0 else W // 2
    rt = 512
    pieces = R // (2 * cw)
    nch = W // cw
    nb = R // LANES
    f32, bf16 = jnp.float32, jnp.bfloat16
    anywhere = pl.BlockSpec(memory_space=pl.ANY)
    vmem = pl.BlockSpec(memory_space=pltpu.VMEM)
    dma = pltpu.SemaphoreType.DMA
    peers = max(n_dp, n_row, n_col) - 1
    g, _, xt, wgs, ra, cb, row_stats, col_stats = pl.pallas_call(
        functools.partial(gather_kernel, (n_dp, n_row, n_col, cw, rt)),
        out_shape=[
            jax.ShapeDtypeStruct((tokens, W), bf16),
            jax.ShapeDtypeStruct((tokens, R), bf16),
            jax.ShapeDtypeStruct((R, tokens), bf16),
            jax.ShapeDtypeStruct((R, W // 2), f32),
            jax.ShapeDtypeStruct((R, LANES), f32),
            jax.ShapeDtypeStruct((1, W), f32),
            jax.ShapeDtypeStruct((nb, LANES), f32),
            jax.ShapeDtypeStruct((1, W), f32),
        ],
        in_specs=[anywhere, anywhere, vmem, vmem],
        out_specs=[anywhere] * 4 + [vmem] * 4,
        scratch_shapes=[
            pltpu.VMEM((R, tokens), bf16),
            pltpu.VMEM((tokens, 2 * cw), bf16),
            pltpu.VMEM((nch // 2, R, cw), f32),
            pltpu.VMEM((2, R // 2, cw), f32),
            pltpu.VMEM((8, W), f32),
            pltpu.VMEM((n_dp, nb, LANES), f32),
            pltpu.VMEM((n_col, nb, LANES), f32),
            pltpu.VMEM((n_row, 1, W), f32),
            pltpu.VMEM((n_dp, 8, LANES), f32),
            pltpu.VMEM((n_row, 16, LANES), f32),
            pltpu.VMEM((n_col, 8, LANES), f32),
            dma((nch, n_dp - 1)), dma((nch, n_dp - 1)), dma((nch, n_dp - 1)), dma((nch, n_dp - 1)),
            dma((pieces, n_dp - 1)), dma((pieces, n_dp - 1)),
            dma((pieces * n_dp, n_col - 1)), dma((pieces * n_dp, n_col - 1)),
            dma((6, peers)), dma((6, peers)),
            dma((3,)), dma((2,)), dma((1,)),
        ],
        compiler_params=pltpu.CompilerParams(
            collective_id=0, has_side_effects=True, vmem_limit_bytes=60 * 1024 * 1024),
        cost_estimate=pl.CostEstimate(flops=2 * R * W * tokens, bytes_accessed=8 * R * W, transcendentals=0),
        name="exchange_and_stats",
    )(tokens_in, out_grad, row_state.reshape(nb, LANES), col_state.reshape(1, W))

    frt = 1024
    update = pl.pallas_call(
        finish_kernel,
        out_shape=jax.ShapeDtypeStruct((R, W), f32),
        grid=(nch // 2, R // frt),
        in_specs=[
            pl.BlockSpec(memory_space=pltpu.VMEM),
            pl.BlockSpec((tokens, cw), lambda p, r: (0, 2 * p + 1)),
            pl.BlockSpec((frt, cw), lambda p, r: (r, p)),
            pl.BlockSpec((frt, LANES), lambda p, r: (r, 0)),
            pl.BlockSpec((1, 2 * cw), lambda p, r: (0, p)),
        ],
        out_specs=pl.BlockSpec((frt, 2 * cw), lambda p, r: (r, p)),
        compiler_params=pltpu.CompilerParams(vmem_limit_bytes=48 * 1024 * 1024),
        cost_estimate=pl.CostEstimate(flops=R * W * tokens, bytes_accessed=6 * R * W, transcendentals=0),
        name="scaled_update",
    )(xt, g, wgs, ra, cb)
    return update, row_stats.reshape(R), col_stats.reshape(W)


def solution(mesh):
    sizes = (mesh.shape["dp"], mesh.shape["row"], mesh.shape["col"])
    return jax.shard_map(
        functools.partial(on_device, sizes),
        mesh=mesh,
        in_specs=(P(("dp", "col"), "row"), P("dp", "col"), P("row"), P(("col", "dp"))),
        out_specs=(P("row", ("col", "dp")), P("row"), P(("col", "dp"))),
        check_vma=False,
    )
```

```python
import functools

import jax
import jax.numpy as jnp
from jax import lax
from jax.experimental import pallas as pl
from jax.experimental.pallas import tpu as pltpu
from jax.sharding import PartitionSpec as P

MESH = pl.DeviceIdType.MESH
DECAY = 0.7
CLIP = 1.0
LANES = 128
AHEAD = 3


def gather_kernel(sizes, tok_ref, og_ref, rstate_ref, cstate_ref,
                  g_ref, x_ref, xt_out, wgs_ref, ra_ref, cb_ref, rstat_ref, cstat_ref,
                  xt, gbuf, hold, stage, colacc, rslot, r2slot, cslot, pslot, qslot, p2slot,
                  xs, xr, zs, zr, ts, tr, us, ur, es, er, lsem, stsem, gsem):
    n_dp, n_row, n_col, cw, rt = sizes
    assert n_dp == 4 and n_row % 2 == 0
    R = xt.shape[0]
    W = g_ref.shape[1]
    T = og_ref.shape[0]
    half = T // 2
    tb = tok_ref.shape[0]
    nch = W // cw
    groups = cw // LANES
    wide = 2 * cw
    pieces = R // wide
    shared = nch - nch // 6
    dp, row, col = lax.axis_index("dp"), lax.axis_index("row"), lax.axis_index("col")
    h = row % 2
    mate = row + 1 - 2 * h

    def peer(i, d, n):
        return lax.rem(i + d, n)

    def origin(i, d, n):
        return lax.rem(i + n - d, n)

    def mul(v, m):
        return pl.multiple_of(v * m, m)

    barrier = pltpu.get_barrier_semaphore()
    for axis, me, n in (("dp", dp, n_dp), ("row", row, n_row), ("col", col, n_col)):
        for d in range(1, n):
            pl.semaphore_signal(barrier, inc=1, device_id={axis: peer(me, d, n)}, device_id_type=MESH)
    pl.semaphore_wait(barrier, n_dp + n_row + n_col - 3)

    def xy(k, d, part, ss, rs):
        to = peer(dp, d, n_dp)
        return pltpu.make_async_remote_copy(
            src_ref=og_ref.at[pl.ds(mul(part, half), half), pl.ds(pl.multiple_of(to * W + k * cw, LANES), cw)],
            dst_ref=g_ref.at[pl.ds(pl.multiple_of(dp * T + part * half, half), half), pl.ds(mul(k, cw), cw)],
            send_sem=ss.at[k, d - 1], recv_sem=rs.at[k, d - 1],
            device_id={"dp": to}, device_id_type=MESH)

    def block(k, d, part):
        frm = origin(dp, d, n_dp)
        return g_ref.at[pl.ds(pl.multiple_of(frm * T + part * half, half), half), pl.ds(mul(k, cw), cw)]

    def xy_in(k, d):
        ref = block(k, d, h)
        return pltpu.make_async_remote_copy(
            src_ref=ref, dst_ref=ref, send_sem=xs.at[k, d - 1], recv_sem=xr.at[k, d - 1],
            device_id={"dp": origin(dp, d, n_dp)}, device_id_type=MESH)

    def zcopy(k, d, part):
        ref = block(k, d, part)
        return pltpu.make_async_remote_copy(
            src_ref=ref, dst_ref=ref, send_sem=zs.at[k, d - 1], recv_sem=zr.at[k, d - 1],
            device_id={"row": mate}, device_id_type=MESH)

    def send_xy(k):
        for d in range(1, n_dp):
            xy(k, d, h, xs, xr).start()

        @pl.when(k >= shared)
        def _():
            for d in range(1, n_dp):
                xy(k, d, 1 - h, zs, zr).start()

    def forward(k):
        for d in range(1, n_dp):
            xy_in(k, d).wait_recv()
            zcopy(k, d, h).start()

    def tokens_at(i, c, q):
        return x_ref.at[pl.ds(mul(i * n_col + c, tb), tb), pl.ds(q * wide, wide)]

    def tok_piece(q):
        return tok_ref.at[:, pl.ds(q * wide, wide)]

    side, over = dp + 1 - 2 * (dp % 2), (dp + 2) % 4
    owners = (dp, side, over, (side + 2) % 4)

    def tok_dp(q, i, owner):
        if i < 2:
            src, dst = tok_piece(q), tokens_at(owner, col, q)
        else:
            src = dst = x_ref.at[pl.ds(mul(owner * n_col + col, tb), tb), pl.ds(q * wide + (i - 2) * cw, cw)]
        return pltpu.make_async_remote_copy(
            src_ref=src, dst_ref=dst, send_sem=ts.at[q, i], recv_sem=tr.at[q, i],
            device_id={"dp": (side, over, over, side)[i]}, device_id_type=MESH)

    def tok_col(q, d, e, c):
        ref = tokens_at(owners[d], c, q)
        return pltpu.make_async_remote_copy(
            src_ref=tok_piece(q) if d == 0 else ref, dst_ref=ref,
            send_sem=us.at[q * n_dp + d, e - 1], recv_sem=ur.at[q * n_dp + d, e - 1],
            device_id={"col": peer(col, e, n_col)}, device_id_type=MESH)

    def send_tok(q):
        for i in range(2):
            tok_dp(q, i, dp).start()
        for e in range(1, n_col):
            tok_col(q, 0, e, col).start()

    def pass_tok(q):
        for i in range(2):
            tok_dp(q, i, owners[1 + i]).wait_recv()
            tok_dp(q, 2 + i, owners[1 + i]).start()
            for e in range(1, n_col):
                tok_col(q, 1 + i, e, col).start()

    def corner_tok(q):
        for i in range(2, 4):
            tok_dp(q, i, owners[3]).wait_recv()
        for e in range(1, n_col):
            tok_col(q, 3, e, col).start()

    send_xy(0)
    own_tok = pltpu.make_async_copy(tok_ref, x_ref.at[pl.ds(mul(dp * n_col + col, tb), tb), :], lsem.at[0])
    own_tok.start()
    send_tok(0)
    own_grad = pltpu.make_async_copy(
        og_ref.at[:, pl.ds(mul(dp, W), W)], g_ref.at[pl.ds(mul(dp, T), T), :], lsem.at[1])
    own_grad.start()
    if nch > 1:
        send_xy(1)

    ra_ref[...] = jnp.zeros_like(ra_ref)
    colacc[...] = jnp.zeros_like(colacc)

    def turn_tok(q):
        for d in range(n_dp):
            for e in range(1, n_col):
                tok_col(q, d, e, origin(col, e, n_col)).wait_recv()
        load = pltpu.make_async_copy(x_ref.at[:, pl.ds(q * wide, wide)], gbuf, gsem.at[0])
        load.start()
        load.wait()
        for part in range(wide // LANES):
            xt[q * wide + part * LANES:q * wide + (part + 1) * LANES, :] = (
                gbuf[:, part * LANES:(part + 1) * LANES].T)

    sent = min(2, nch)
    own_tok.wait()
    for q in range(pieces):
        if q + 1 < pieces:
            send_tok(q + 1)
        if q > 0:
            corner_tok(q - 1)
        if q < min(AHEAD, shared):
            forward(q)
        if sent < nch:
            send_xy(sent)
            sent += 1
        pass_tok(q)
        if q > 0:
            turn_tok(q - 1)
    for q in range(pieces, min(AHEAD, shared)):
        forward(q)
    for _ in range(2):
        if sent < nch:
            send_xy(sent)
            sent += 1
    corner_tok(pieces - 1)
    turn_tok(pieces - 1)

    out_xt = pltpu.make_async_copy(xt, xt_out, lsem.at[2])
    out_xt.start()
    own_grad.wait()

    def work(p):
        load = pltpu.make_async_copy(g_ref.at[:, pl.ds(mul(p, wide), wide)], gbuf, gsem.at[0])
        load.start()
        load.wait()
        columns = pl.ds(mul(p, wide), wide)

        @pl.loop(0, R // rt)
        def _(r):
            rows = pl.ds(mul(r, rt), rt)
            w = jnp.dot(xt[rows, :], gbuf[...], preferred_element_type=jnp.float32)
            stage[r // tiles, pl.ds(mul(r % tiles, rt), rt), :] = w[:, :cw]
            hold[p, rows, :] = w[:, cw:]
            sq = w * w
            part = sq[:, :LANES]
            for j in range(1, 2 * groups):
                part = part + sq[:, j * LANES:(j + 1) * LANES]
            ra_ref[rows, :] += part
            colacc[:, columns] += jnp.sum(sq.reshape(rt // 8, 8, wide), axis=0)

    def arrive(p):
        for i in range(2):
            k = 2 * p + i

            @pl.when(k + sent < nch)
            def _():
                send_xy(k + sent)

            @pl.when(k + AHEAD < shared)
            def _():
                forward(k + AHEAD)

        for i in range(2):
            k = 2 * p + i
            for d in range(1, n_dp):
                zcopy(k, d, 1 - h).wait_recv()

            @pl.when(k >= shared)
            def _():
                for d in range(1, n_dp):
                    xy_in(k, d).wait_recv()

    tiles = R // 2 // rt

    def store_out(p, s):
        return pltpu.make_async_copy(
            stage.at[s], wgs_ref.at[pl.ds(s * (R // 2), R // 2), pl.ds(mul(p, cw), cw)], stsem.at[s])

    def load_back(p, s):
        return pltpu.make_async_copy(
            wgs_ref.at[pl.ds(s * (R // 2), R // 2), pl.ds(mul(p, cw), cw)], stage.at[s], stsem.at[s])

    @pl.loop(0, nch // 2)
    def _(p):
        arrive(p)

        @pl.when(p > 0)
        def _():
            for s in range(2):
                store_out(p - 1, s).wait()

        work(p)
        for s in range(2):
            store_out(p, s).start()

    def exchange(axis, me, n, slots, row_no):
        out = []
        for d in range(1, n):
            c = pltpu.make_async_remote_copy(
                src_ref=slots.at[me], dst_ref=slots.at[me], send_sem=es.at[row_no, d - 1],
                recv_sem=er.at[row_no, d - 1], device_id={axis: peer(me, d, n)}, device_id_type=MESH)
            c.start()
            out.append(c)

        def finish():
            for d in range(1, n):
                ref = slots.at[origin(me, d, n)]
                out[d - 1].wait_send()
                pltpu.make_async_remote_copy(
                    src_ref=ref, dst_ref=ref, send_sem=es.at[row_no, d - 1], recv_sem=er.at[row_no, d - 1],
                    device_id={axis: peer(me, d, n)}, device_id_type=MESH).wait_recv()
            total = slots[0]
            for i in range(1, n):
                total = total + slots[i]
            return total

        return finish

    nb = R // LANES
    cslot[row] = jnp.sum(colacc[...], axis=0, keepdims=True)
    finish_col = exchange("row", row, n_row, cslot, 0)
    for b in range(nb):
        rslot[dp, b:b + 1, :] = jnp.sum(ra_ref[b * LANES:(b + 1) * LANES, :].T, axis=0, keepdims=True)
    r2slot[col] = exchange("dp", dp, n_dp, rslot, 1)()
    row_sum = exchange("col", col, n_col, r2slot, 2)()
    row_stats = DECAY * rstate_ref[...] + (1.0 - DECAY) * (row_sum / (W * n_dp * n_col))
    rstat_ref[...] = row_stats
    local_mean = jnp.sum(row_stats) / R
    scale = lax.rsqrt(row_stats / local_mean)
    for b in range(nb):
        ra_ref[b * LANES:(b + 1) * LANES, :] = jnp.broadcast_to(scale[b:b + 1, :], (LANES, LANES)).T
    col_stats = DECAY * cstate_ref[...] + (1.0 - DECAY) * (finish_col() / (R * n_row))
    cstat_ref[...] = col_stats
    cb_ref[...] = lax.rsqrt(col_stats)

    for s in range(2):
        store_out(nch // 2 - 1, s).wait()
    pslot[dp] = jnp.zeros((8, LANES), jnp.float32)

    def power(read, first, count, k):
        columns = pl.ds(mul(k, cw), cw)
        cb = cb_ref[:, columns]

        @pl.loop(0, count)
        def _(r):
            a = ra_ref[pl.ds(pl.multiple_of(first + r * rt, rt), rt), :]
            w = read(r)
            acc = jnp.zeros((8, LANES), jnp.float32)
            for j in range(groups):
                u = w[:, j * LANES:(j + 1) * LANES] * a * cb[:, j * LANES:(j + 1) * LANES]
                acc = acc + jnp.sum((u * u).reshape(rt // 8, 8, LANES), axis=0)
            pslot[dp] += acc

    last = nch // 2 - 1

    def staged(s, p):
        power(lambda r: stage[s, pl.ds(mul(r, rt), rt), :], s * (R // 2), tiles, 2 * p)

    def held(p):
        power(lambda r: hold[p, pl.ds(mul(r, rt), rt), :], 0, R // rt, 2 * p + 1)

    for s in range(2):
        staged(s, last)
        if last > 0:
            load_back(0, s).start()

    @pl.loop(0, last)
    def _(p):
        held(p)
        for s in range(2):
            load_back(p, s).wait()
            staged(s, p)

            @pl.when(p + 1 < last)
            def _():
                load_back(p + 1, s).start()

    held(last)
    qslot[row, 0:8, :] = exchange("dp", dp, n_dp, pslot, 3)()
    qslot[row, 8:16, :] = jnp.full((8, LANES), local_mean, jnp.float32)
    exchange("row", row, n_row, qslot, 4)()
    mean = qslot[0, 8:16, :]
    for i in range(1, n_row):
        mean = mean + qslot[i, 8:16, :]
    mean = mean / n_row
    total = qslot[0, 0:8, :] * (mean / qslot[0, 8:16, :])
    for i in range(1, n_row):
        total = total + qslot[i, 0:8, :] * (mean / qslot[i, 8:16, :])
    p2slot[col] = total
    power_mean = jnp.sum(exchange("col", col, n_col, p2slot, 5)()) / (R * n_row * W * n_dp * n_col)
    tail = jnp.full((1, LANES), power_mean, jnp.float32)
    clip = jnp.maximum(1.0, jnp.sqrt(tail) / CLIP)
    factor = jnp.sqrt(mean[0:1, :] / local_mean) / clip
    for j in range(W // LANES):
        cb_ref[:, j * LANES:(j + 1) * LANES] = cb_ref[:, j * LANES:(j + 1) * LANES] * factor

    out_xt.wait()
    for q in range(pieces):
        for i in range(4):
            tok_dp(q, i, dp if i < 2 else owners[i - 1]).wait_send()
        for d in range(n_dp):
            for e in range(1, n_col):
                tok_col(q, d, e, col).wait_send()

    @pl.loop(0, nch)
    def _(k):
        for d in range(1, n_dp):
            xy(k, d, h, xs, xr).wait_send()
            zcopy(k, d, h).wait_send()


def finish_kernel(xt_ref, g_ref, w_ref, ra_ref, cb_ref, out_ref):
    rows, cw = w_ref.shape
    r = pl.program_id(1)
    a = ra_ref[...]
    cb = cb_ref[...]
    x = xt_ref[pl.ds(pl.multiple_of(r * rows, rows), rows), :]
    w = jnp.dot(x, g_ref[...], preferred_element_type=jnp.float32)
    for j in range(cw // LANES):
        s = slice(j * LANES, (j + 1) * LANES)
        out_ref[:, s] = w_ref[:, s] * a * cb[:, s]
        s2 = slice(cw + j * LANES, cw + (j + 1) * LANES)
        out_ref[:, s2] = w[:, s] * a * cb[:, s2]


def on_device(sizes, tokens_in, out_grad, row_state, col_state):
    n_dp, n_row, n_col = sizes
    tb, R = tokens_in.shape
    T, wide = out_grad.shape
    W = wide // n_dp
    tokens = T * n_dp
    cw = 512 if W % 1024 == 0 else W // 2
    rt = 512
    pieces = R // (2 * cw)
    nch = W // cw
    nb = R // LANES
    f32, bf16 = jnp.float32, jnp.bfloat16
    anywhere = pl.BlockSpec(memory_space=pl.ANY)
    vmem = pl.BlockSpec(memory_space=pltpu.VMEM)
    dma = pltpu.SemaphoreType.DMA
    peers = max(n_dp, n_row, n_col) - 1
    g, _, xt, wgs, ra, cb, row_stats, col_stats = pl.pallas_call(
        functools.partial(gather_kernel, (n_dp, n_row, n_col, cw, rt)),
        out_shape=[
            jax.ShapeDtypeStruct((tokens, W), bf16),
            jax.ShapeDtypeStruct((tokens, R), bf16),
            jax.ShapeDtypeStruct((R, tokens), bf16),
            jax.ShapeDtypeStruct((R, W // 2), f32),
            jax.ShapeDtypeStruct((R, LANES), f32),
            jax.ShapeDtypeStruct((1, W), f32),
            jax.ShapeDtypeStruct((nb, LANES), f32),
            jax.ShapeDtypeStruct((1, W), f32),
        ],
        in_specs=[anywhere, anywhere, vmem, vmem],
        out_specs=[anywhere] * 4 + [vmem] * 4,
        scratch_shapes=[
            pltpu.VMEM((R, tokens), bf16),
            pltpu.VMEM((tokens, 2 * cw), bf16),
            pltpu.VMEM((nch // 2, R, cw), f32),
            pltpu.VMEM((2, R // 2, cw), f32),
            pltpu.VMEM((8, W), f32),
            pltpu.VMEM((n_dp, nb, LANES), f32),
            pltpu.VMEM((n_col, nb, LANES), f32),
            pltpu.VMEM((n_row, 1, W), f32),
            pltpu.VMEM((n_dp, 8, LANES), f32),
            pltpu.VMEM((n_row, 16, LANES), f32),
            pltpu.VMEM((n_col, 8, LANES), f32),
            dma((nch, n_dp - 1)), dma((nch, n_dp - 1)), dma((nch, n_dp - 1)), dma((nch, n_dp - 1)),
            dma((pieces, 4)), dma((pieces, 4)),
            dma((pieces * n_dp, n_col - 1)), dma((pieces * n_dp, n_col - 1)),
            dma((6, peers)), dma((6, peers)),
            dma((3,)), dma((2,)), dma((1,)),
        ],
        compiler_params=pltpu.CompilerParams(
            collective_id=0, has_side_effects=True, vmem_limit_bytes=60 * 1024 * 1024),
        cost_estimate=pl.CostEstimate(flops=2 * R * W * tokens, bytes_accessed=8 * R * W, transcendentals=0),
        name="exchange_and_stats",
    )(tokens_in, out_grad, row_state.reshape(nb, LANES), col_state.reshape(1, W))

    frt = 1024
    update = pl.pallas_call(
        finish_kernel,
        out_shape=jax.ShapeDtypeStruct((R, W), f32),
        grid=(nch // 2, R // frt),
        in_specs=[
            pl.BlockSpec(memory_space=pltpu.VMEM),
            pl.BlockSpec((tokens, cw), lambda p, r: (0, 2 * p + 1)),
            pl.BlockSpec((frt, cw), lambda p, r: (r, p)),
            pl.BlockSpec((frt, LANES), lambda p, r: (r, 0)),
            pl.BlockSpec((1, 2 * cw), lambda p, r: (0, p)),
        ],
        out_specs=pl.BlockSpec((frt, 2 * cw), lambda p, r: (r, p)),
        compiler_params=pltpu.CompilerParams(vmem_limit_bytes=48 * 1024 * 1024),
        cost_estimate=pl.CostEstimate(flops=R * W * tokens, bytes_accessed=6 * R * W, transcendentals=0),
        name="scaled_update",
    )(xt, g, wgs, ra, cb)
    return update, row_stats.reshape(R), col_stats.reshape(W)


def solution(mesh):
    sizes = (mesh.shape["dp"], mesh.shape["row"], mesh.shape["col"])
    return jax.shard_map(
        functools.partial(on_device, sizes),
        mesh=mesh,
        in_specs=(P(("dp", "col"), "row"), P("dp", "col"), P("row"), P(("col", "dp"))),
        out_specs=(P("row", ("col", "dp")), P("row"), P(("col", "dp"))),
        check_vma=False,
    )
```

```python
import functools

import jax
import jax.numpy as jnp
from jax import lax
from jax.experimental import pallas as pl
from jax.experimental.pallas import tpu as pltpu
from jax.sharding import PartitionSpec as P

MESH = pl.DeviceIdType.MESH
DECAY = 0.7
CLIP = 1.0
LANES = 128
AHEAD = 3


def gather_kernel(sizes, tok_ref, og_ref, rstate_ref, cstate_ref,
                  g_ref, x_ref, xt_out, wgs_ref, ra_ref, cb_ref, rstat_ref, cstat_ref,
                  xt, gbuf, hold, stage, colacc, rslot, r2slot, cslot, pslot, qslot, p2slot,
                  xs, xr, zs, zr, ts, tr, us, ur, es, er, lsem, stsem, gsem):
    n_dp, n_row, n_col, cw, rt = sizes
    assert n_dp == 4 and n_row % 2 == 0
    R = xt.shape[0]
    W = g_ref.shape[1]
    T = og_ref.shape[0]
    half = T // 2
    tb = tok_ref.shape[0]
    nch = W // cw
    groups = cw // LANES
    wide = 2 * cw
    pieces = R // wide
    shared = nch - nch // 3
    dp, row, col = lax.axis_index("dp"), lax.axis_index("row"), lax.axis_index("col")
    h = row % 2
    mate = row + 1 - 2 * h

    def peer(i, d, n):
        return lax.rem(i + d, n)

    def origin(i, d, n):
        return lax.rem(i + n - d, n)

    def mul(v, m):
        return pl.multiple_of(v * m, m)

    barrier = pltpu.get_barrier_semaphore()
    for axis, me, n in (("dp", dp, n_dp), ("row", row, n_row), ("col", col, n_col)):
        for d in range(1, n):
            pl.semaphore_signal(barrier, inc=1, device_id={axis: peer(me, d, n)}, device_id_type=MESH)
    pl.semaphore_wait(barrier, n_dp + n_row + n_col - 3)

    def xy(k, d, part, ss, rs):
        to = peer(dp, d, n_dp)
        return pltpu.make_async_remote_copy(
            src_ref=og_ref.at[pl.ds(mul(part, half), half), pl.ds(pl.multiple_of(to * W + k * cw, LANES), cw)],
            dst_ref=g_ref.at[pl.ds(pl.multiple_of(dp * T + part * half, half), half), pl.ds(mul(k, cw), cw)],
            send_sem=ss.at[k, d - 1], recv_sem=rs.at[k, d - 1],
            device_id={"dp": to}, device_id_type=MESH)

    def block(k, d, part):
        frm = origin(dp, d, n_dp)
        return g_ref.at[pl.ds(pl.multiple_of(frm * T + part * half, half), half), pl.ds(mul(k, cw), cw)]

    def xy_in(k, d):
        ref = block(k, d, h)
        return pltpu.make_async_remote_copy(
            src_ref=ref, dst_ref=ref, send_sem=xs.at[k, d - 1], recv_sem=xr.at[k, d - 1],
            device_id={"dp": origin(dp, d, n_dp)}, device_id_type=MESH)

    def zcopy(k, d, part):
        ref = block(k, d, part)
        return pltpu.make_async_remote_copy(
            src_ref=ref, dst_ref=ref, send_sem=zs.at[k, d - 1], recv_sem=zr.at[k, d - 1],
            device_id={"row": mate}, device_id_type=MESH)

    def send_xy(k):
        for d in range(1, n_dp):
            xy(k, d, h, xs, xr).start()

        @pl.when(k >= shared)
        def _():
            for d in range(1, n_dp):
                xy(k, d, 1 - h, zs, zr).start()

    def forward(k):
        for d in range(1, n_dp):
            xy_in(k, d).wait_recv()
            zcopy(k, d, h).start()

    def tokens_at(i, c, q):
        return x_ref.at[pl.ds(mul(i * n_col + c, tb), tb), pl.ds(q * wide, wide)]

    def tok_piece(q):
        return tok_ref.at[:, pl.ds(q * wide, wide)]

    side, over = dp + 1 - 2 * (dp % 2), (dp + 2) % 4
    owners = (dp, side, over, (side + 2) % 4)

    def tok_dp(q, i, owner):
        if i < 2:
            src, dst = tok_piece(q), tokens_at(owner, col, q)
        else:
            src = dst = x_ref.at[pl.ds(mul(owner * n_col + col, tb), tb), pl.ds(q * wide + (i - 2) * cw, cw)]
        return pltpu.make_async_remote_copy(
            src_ref=src, dst_ref=dst, send_sem=ts.at[q, i], recv_sem=tr.at[q, i],
            device_id={"dp": (side, over, over, side)[i]}, device_id_type=MESH)

    def tok_col(q, d, e, c):
        ref = tokens_at(owners[d], c, q)
        return pltpu.make_async_remote_copy(
            src_ref=tok_piece(q) if d == 0 else ref, dst_ref=ref,
            send_sem=us.at[q * n_dp + d, e - 1], recv_sem=ur.at[q * n_dp + d, e - 1],
            device_id={"col": peer(col, e, n_col)}, device_id_type=MESH)

    def send_tok(q):
        for i in range(2):
            tok_dp(q, i, dp).start()
        for e in range(1, n_col):
            tok_col(q, 0, e, col).start()

    def pass_tok(q):
        for i in range(2):
            tok_dp(q, i, owners[1 + i]).wait_recv()
            tok_dp(q, 2 + i, owners[1 + i]).start()
            for e in range(1, n_col):
                tok_col(q, 1 + i, e, col).start()

    def corner_tok(q):
        for i in range(2, 4):
            tok_dp(q, i, owners[3]).wait_recv()
        for e in range(1, n_col):
            tok_col(q, 3, e, col).start()

    send_xy(0)
    own_tok = pltpu.make_async_copy(tok_ref, x_ref.at[pl.ds(mul(dp * n_col + col, tb), tb), :], lsem.at[0])
    own_tok.start()
    for q in range(pieces):
        send_tok(q)
    own_grad = pltpu.make_async_copy(
        og_ref.at[:, pl.ds(mul(dp, W), W)], g_ref.at[pl.ds(mul(dp, T), T), :], lsem.at[1])
    own_grad.start()
    if nch > 1:
        send_xy(1)

    ra_ref[...] = jnp.zeros_like(ra_ref)
    colacc[...] = jnp.zeros_like(colacc)

    def turn_tok(q):
        for d in range(n_dp):
            for e in range(1, n_col):
                tok_col(q, d, e, origin(col, e, n_col)).wait_recv()
        load = pltpu.make_async_copy(x_ref.at[:, pl.ds(q * wide, wide)], gbuf, gsem.at[0])
        load.start()
        load.wait()
        for part in range(wide // LANES):
            xt[q * wide + part * LANES:q * wide + (part + 1) * LANES, :] = (
                gbuf[:, part * LANES:(part + 1) * LANES].T)

    sent = min(2, nch)
    own_tok.wait()
    forward(0)
    if sent < nch:
        send_xy(sent)
        sent += 1
    for q in range(pieces):
        if q > 0:
            corner_tok(q - 1)
        pass_tok(q)
        if q > 0:
            turn_tok(q - 1)
            if sent < nch:
                send_xy(sent)
                sent += 1
            if q < min(AHEAD, shared):
                forward(q)
    for q in range(pieces, min(AHEAD, shared)):
        forward(q)
    for _ in range(2):
        if sent < nch:
            send_xy(sent)
            sent += 1
    corner_tok(pieces - 1)
    turn_tok(pieces - 1)

    out_xt = pltpu.make_async_copy(xt, xt_out, lsem.at[2])
    out_xt.start()
    own_grad.wait()

    def work(p):
        load = pltpu.make_async_copy(g_ref.at[:, pl.ds(mul(p, wide), wide)], gbuf, gsem.at[0])
        load.start()
        load.wait()
        columns = pl.ds(mul(p, wide), wide)

        @pl.loop(0, R // rt)
        def _(r):
            rows = pl.ds(mul(r, rt), rt)
            w = jnp.dot(xt[rows, :], gbuf[...], preferred_element_type=jnp.float32)
            stage[r // tiles, pl.ds(mul(r % tiles, rt), rt), :] = w[:, :cw]
            hold[p, rows, :] = w[:, cw:]
            sq = w * w
            part = sq[:, :LANES]
            for j in range(1, 2 * groups):
                part = part + sq[:, j * LANES:(j + 1) * LANES]
            ra_ref[rows, :] += part
            colacc[:, columns] += jnp.sum(sq.reshape(rt // 8, 8, wide), axis=0)

    def arrive(p):
        for i in range(2):
            k = 2 * p + i

            @pl.when(k + sent < nch)
            def _():
                send_xy(k + sent)

            @pl.when(k + AHEAD < shared)
            def _():
                forward(k + AHEAD)

        for i in range(2):
            k = 2 * p + i
            for d in range(1, n_dp):
                zcopy(k, d, 1 - h).wait_recv()

            @pl.when(k >= shared)
            def _():
                for d in range(1, n_dp):
                    xy_in(k, d).wait_recv()

    tiles = R // 2 // rt

    def store_out(p, s):
        return pltpu.make_async_copy(
            stage.at[s], wgs_ref.at[pl.ds(s * (R // 2), R // 2), pl.ds(mul(p, cw), cw)], stsem.at[s])

    def load_back(p, s):
        return pltpu.make_async_copy(
            wgs_ref.at[pl.ds(s * (R // 2), R // 2), pl.ds(mul(p, cw), cw)], stage.at[s], stsem.at[s])

    @pl.loop(0, nch // 2)
    def _(p):
        arrive(p)

        @pl.when(p > 0)
        def _():
            for s in range(2):
                store_out(p - 1, s).wait()

        work(p)
        for s in range(2):
            store_out(p, s).start()

    def exchange(axis, me, n, slots, row_no):
        out = []
        for d in range(1, n):
            c = pltpu.make_async_remote_copy(
                src_ref=slots.at[me], dst_ref=slots.at[me], send_sem=es.at[row_no, d - 1],
                recv_sem=er.at[row_no, d - 1], device_id={axis: peer(me, d, n)}, device_id_type=MESH)
            c.start()
            out.append(c)

        def finish():
            for d in range(1, n):
                ref = slots.at[origin(me, d, n)]
                out[d - 1].wait_send()
                pltpu.make_async_remote_copy(
                    src_ref=ref, dst_ref=ref, send_sem=es.at[row_no, d - 1], recv_sem=er.at[row_no, d - 1],
                    device_id={axis: peer(me, d, n)}, device_id_type=MESH).wait_recv()
            total = slots[0]
            for i in range(1, n):
                total = total + slots[i]
            return total

        return finish

    nb = R // LANES
    cslot[row] = jnp.sum(colacc[...], axis=0, keepdims=True)
    finish_col = exchange("row", row, n_row, cslot, 0)
    for b in range(nb):
        rslot[dp, b:b + 1, :] = jnp.sum(ra_ref[b * LANES:(b + 1) * LANES, :].T, axis=0, keepdims=True)
    r2slot[col] = exchange("dp", dp, n_dp, rslot, 1)()
    row_sum = exchange("col", col, n_col, r2slot, 2)()
    row_stats = DECAY * rstate_ref[...] + (1.0 - DECAY) * (row_sum / (W * n_dp * n_col))
    rstat_ref[...] = row_stats
    local_mean = jnp.sum(row_stats) / R
    scale = lax.rsqrt(row_stats / local_mean)
    for b in range(nb):
        ra_ref[b * LANES:(b + 1) * LANES, :] = jnp.broadcast_to(scale[b:b + 1, :], (LANES, LANES)).T
    col_stats = DECAY * cstate_ref[...] + (1.0 - DECAY) * (finish_col() / (R * n_row))
    cstat_ref[...] = col_stats
    cb_ref[...] = lax.rsqrt(col_stats)

    for s in range(2):
        store_out(nch // 2 - 1, s).wait()
    pslot[dp] = jnp.zeros((8, LANES), jnp.float32)

    def power(read, first, count, k):
        columns = pl.ds(mul(k, cw), cw)
        cb = cb_ref[:, columns]

        @pl.loop(0, count)
        def _(r):
            a = ra_ref[pl.ds(pl.multiple_of(first + r * rt, rt), rt), :]
            w = read(r)
            acc = jnp.zeros((8, LANES), jnp.float32)
            for j in range(groups):
                u = w[:, j * LANES:(j + 1) * LANES] * a * cb[:, j * LANES:(j + 1) * LANES]
                acc = acc + jnp.sum((u * u).reshape(rt // 8, 8, LANES), axis=0)
            pslot[dp] += acc

    last = nch // 2 - 1

    def staged(s, p):
        power(lambda r: stage[s, pl.ds(mul(r, rt), rt), :], s * (R // 2), tiles, 2 * p)

    def held(p):
        power(lambda r: hold[p, pl.ds(mul(r, rt), rt), :], 0, R // rt, 2 * p + 1)

    for s in range(2):
        staged(s, last)
        if last > 0:
            load_back(0, s).start()

    @pl.loop(0, last)
    def _(p):
        held(p)
        for s in range(2):
            load_back(p, s).wait()
            staged(s, p)

            @pl.when(p + 1 < last)
            def _():
                load_back(p + 1, s).start()

    held(last)
    qslot[row, 0:8, :] = exchange("dp", dp, n_dp, pslot, 3)()
    qslot[row, 8:16, :] = jnp.full((8, LANES), local_mean, jnp.float32)
    exchange("row", row, n_row, qslot, 4)()
    mean = qslot[0, 8:16, :]
    for i in range(1, n_row):
        mean = mean + qslot[i, 8:16, :]
    mean = mean / n_row
    total = qslot[0, 0:8, :] * (mean / qslot[0, 8:16, :])
    for i in range(1, n_row):
        total = total + qslot[i, 0:8, :] * (mean / qslot[i, 8:16, :])
    p2slot[col] = total
    power_mean = jnp.sum(exchange("col", col, n_col, p2slot, 5)()) / (R * n_row * W * n_dp * n_col)
    tail = jnp.full((1, LANES), power_mean, jnp.float32)
    clip = jnp.maximum(1.0, jnp.sqrt(tail) / CLIP)
    factor = jnp.sqrt(mean[0:1, :] / local_mean) / clip
    for j in range(W // LANES):
        cb_ref[:, j * LANES:(j + 1) * LANES] = cb_ref[:, j * LANES:(j + 1) * LANES] * factor

    out_xt.wait()
    for q in range(pieces):
        for i in range(4):
            tok_dp(q, i, dp if i < 2 else owners[i - 1]).wait_send()
        for d in range(n_dp):
            for e in range(1, n_col):
                tok_col(q, d, e, col).wait_send()

    @pl.loop(0, nch)
    def _(k):
        for d in range(1, n_dp):
            xy(k, d, h, xs, xr).wait_send()
            zcopy(k, d, h).wait_send()


def finish_kernel(xt_ref, g_ref, w_ref, ra_ref, cb_ref, out_ref):
    rows, cw = w_ref.shape
    r = pl.program_id(1)
    a = ra_ref[...]
    cb = cb_ref[...]
    x = xt_ref[pl.ds(pl.multiple_of(r * rows, rows), rows), :]
    w = jnp.dot(x, g_ref[...], preferred_element_type=jnp.float32)
    for j in range(cw // LANES):
        s = slice(j * LANES, (j + 1) * LANES)
        out_ref[:, s] = w_ref[:, s] * a * cb[:, s]
        s2 = slice(cw + j * LANES, cw + (j + 1) * LANES)
        out_ref[:, s2] = w[:, s] * a * cb[:, s2]


def on_device(sizes, tokens_in, out_grad, row_state, col_state):
    n_dp, n_row, n_col = sizes
    tb, R = tokens_in.shape
    T, wide = out_grad.shape
    W = wide // n_dp
    tokens = T * n_dp
    cw = 512 if W % 1024 == 0 else W // 2
    rt = 512
    pieces = R // (2 * cw)
    nch = W // cw
    nb = R // LANES
    f32, bf16 = jnp.float32, jnp.bfloat16
    anywhere = pl.BlockSpec(memory_space=pl.ANY)
    vmem = pl.BlockSpec(memory_space=pltpu.VMEM)
    dma = pltpu.SemaphoreType.DMA
    peers = max(n_dp, n_row, n_col) - 1
    g, _, xt, wgs, ra, cb, row_stats, col_stats = pl.pallas_call(
        functools.partial(gather_kernel, (n_dp, n_row, n_col, cw, rt)),
        out_shape=[
            jax.ShapeDtypeStruct((tokens, W), bf16),
            jax.ShapeDtypeStruct((tokens, R), bf16),
            jax.ShapeDtypeStruct((R, tokens), bf16),
            jax.ShapeDtypeStruct((R, W // 2), f32),
            jax.ShapeDtypeStruct((R, LANES), f32),
            jax.ShapeDtypeStruct((1, W), f32),
            jax.ShapeDtypeStruct((nb, LANES), f32),
            jax.ShapeDtypeStruct((1, W), f32),
        ],
        in_specs=[anywhere, anywhere, vmem, vmem],
        out_specs=[anywhere] * 4 + [vmem] * 4,
        scratch_shapes=[
            pltpu.VMEM((R, tokens), bf16),
            pltpu.VMEM((tokens, 2 * cw), bf16),
            pltpu.VMEM((nch // 2, R, cw), f32),
            pltpu.VMEM((2, R // 2, cw), f32),
            pltpu.VMEM((8, W), f32),
            pltpu.VMEM((n_dp, nb, LANES), f32),
            pltpu.VMEM((n_col, nb, LANES), f32),
            pltpu.VMEM((n_row, 1, W), f32),
            pltpu.VMEM((n_dp, 8, LANES), f32),
            pltpu.VMEM((n_row, 16, LANES), f32),
            pltpu.VMEM((n_col, 8, LANES), f32),
            dma((nch, n_dp - 1)), dma((nch, n_dp - 1)), dma((nch, n_dp - 1)), dma((nch, n_dp - 1)),
            dma((pieces, 4)), dma((pieces, 4)),
            dma((pieces * n_dp, n_col - 1)), dma((pieces * n_dp, n_col - 1)),
            dma((6, peers)), dma((6, peers)),
            dma((3,)), dma((2,)), dma((1,)),
        ],
        compiler_params=pltpu.CompilerParams(
            collective_id=0, has_side_effects=True, vmem_limit_bytes=60 * 1024 * 1024),
        cost_estimate=pl.CostEstimate(flops=2 * R * W * tokens, bytes_accessed=8 * R * W, transcendentals=0),
        name="exchange_and_stats",
    )(tokens_in, out_grad, row_state.reshape(nb, LANES), col_state.reshape(1, W))

    frt = 1024
    update = pl.pallas_call(
        finish_kernel,
        out_shape=jax.ShapeDtypeStruct((R, W), f32),
        grid=(nch // 2, R // frt),
        in_specs=[
            pl.BlockSpec(memory_space=pltpu.VMEM),
            pl.BlockSpec((tokens, cw), lambda p, r: (0, 2 * p + 1)),
            pl.BlockSpec((frt, cw), lambda p, r: (r, p)),
            pl.BlockSpec((frt, LANES), lambda p, r: (r, 0)),
            pl.BlockSpec((1, 2 * cw), lambda p, r: (0, p)),
        ],
        out_specs=pl.BlockSpec((frt, 2 * cw), lambda p, r: (r, p)),
        compiler_params=pltpu.CompilerParams(vmem_limit_bytes=48 * 1024 * 1024),
        cost_estimate=pl.CostEstimate(flops=R * W * tokens, bytes_accessed=6 * R * W, transcendentals=0),
        name="scaled_update",
    )(xt, g, wgs, ra, cb)
    return update, row_stats.reshape(R), col_stats.reshape(W)


def solution(mesh):
    sizes = (mesh.shape["dp"], mesh.shape["row"], mesh.shape["col"])
    return jax.shard_map(
        functools.partial(on_device, sizes),
        mesh=mesh,
        in_specs=(P(("dp", "col"), "row"), P("dp", "col"), P("row"), P(("col", "dp"))),
        out_specs=(P("row", ("col", "dp")), P("row"), P(("col", "dp"))),
        check_vma=False,
    )
```
